32 devices in a mesh: dp: 8 (over z, x), fsdp: 4 (over y, core).
Axes of the slice: x: 2, y: 2, z: 4, core: 2. Of those that a mesh axis runs over, the one named last changes fastest.
Arguments:
- tokens: bfloat16 [65536, 1024], P(('dp', 'fsdp')), may hold values from -6 to 6
- in_weight: bfloat16 [1024, 4384], P(('dp', 'fsdp')), may hold values from -0.1875 to 0.1875
- out_weight: bfloat16 [2048, 1024], P(None, ('dp', 'fsdp')), may hold values from -0.125 to 0.125
- conv_weight: bfloat16 [4, 2304], P(None, ('dp', 'fsdp')), may hold values from -3 to 3
- conv_bias: bfloat16 [2304], P(('dp', 'fsdp')), may hold values from -0.5 to 0.5
- norm_gain: bfloat16 [1024], P(('dp', 'fsdp')), may hold values from 0.5 to 1.5
- gate_gain: bfloat16 [2048], P(('dp', 'fsdp')), may hold values from 0.5 to 1.5
- decay_log: float32 [32], P('fsdp'), may hold values from 0 to 2.77
- step_bias: float32 [32], P('fsdp'), may hold values from -6.5 to -2.5
- skip_scale: float32 [32], P('fsdp'), may hold values from 0.5 to 1.5
- cotangent: bfloat16 [65536, 1024], P(('dp', 'fsdp')), may hold values from -6 to 6
Outputs:
- out_tokens: bfloat16 [65536, 1024], P(('dp', 'fsdp'))
- token_grad: bfloat16 [65536, 1024], P(('dp', 'fsdp'))
- in_weight_grad: float32 [1024, 4384], P(('dp', 'fsdp'))
- out_weight_grad: float32 [2048, 1024], P(None, ('dp', 'fsdp'))
- conv_weight_grad: float32 [4, 2304], P(None, ('dp', 'fsdp'))
- conv_bias_grad: float32 [2304], P(('dp', 'fsdp'))
- norm_gain_grad: float32 [1024], P(('dp', 'fsdp'))
- gate_gain_grad: float32 [2048], P(('dp', 'fsdp'))
- decay_log_grad: float32 [32], P('fsdp')
- step_bias_grad: float32 [32], P('fsdp')
- skip_scale_grad: float32 [32], P('fsdp')
The draws below stay inside these ranges and needn't reach their ends.
All inputs are finite; a program needn't handle non-finite values.
Results may differ from the reference program's by a relative error of at most 0.0095.
Values may be sent and summed in bfloat16 or wider, within the bound.
A program may use at most 384 MiB of HBM per device.

```python
import jax
import jax.numpy as jnp
from jax import lax

D = 1024
HEADS = 32
HEADDIM = 64
STATE = 128
KCONV = 4
GROUP = 256
SEQ_LEN = 1024
INNER = 2048
CONVDIM = 2304
PROJ = 4384
TOKENS = 65536


def strengthened(array, key, source, target, parts, factor):
    def block_of(dim):
        return (jnp.arange(array.shape[dim]) // (array.shape[dim] // parts)).reshape((-1,) + (1,) * (array.ndim - 1 - dim))

    first = jax.random.permutation(key, parts)[block_of(target)]
    second = (block_of(target) + parts // 2) % parts
    return jnp.where((block_of(source) == first) | (block_of(source) == second), factor * array, array)


def levels(key, shape, cuts, smallest, high):
    level = 1.0
    for dim, blocks in cuts:
        draws = jax.random.uniform(jax.random.fold_in(jax.random.fold_in(key, 6), dim), (blocks,), jnp.float32, smallest / len(cuts), high / len(cuts))
        level = level * jnp.repeat(jnp.exp(draws), shape[dim] // blocks).reshape((-1,) + (1,) * (len(shape) - 1 - dim))
    return level


def gaussian(stream_key, shape, deviation, most, split=(), held_as=jnp.bfloat16):
    array = jax.random.normal(stream_key, shape, jnp.float32) * deviation
    if len(split) > 0:
        array = levels(stream_key, shape, split, -0.22, 0.18) * array
    return jnp.clip(array, min=-most, max=most).astype(held_as)


def noise_with(own_key, dims, spread, most, split, heavy, held_as=jnp.bfloat16):
    values = spread * jax.random.normal(own_key, dims, jnp.float32)
    if split:
        values = values * levels(own_key, dims, split, -0.22, 0.18)
    return jnp.clip(strengthened(values, jax.random.fold_in(own_key, 3), *heavy), -most, most).astype(held_as)


def setup_inputs(seed: int = 0) -> dict:
    key_list = jax.random.split(jax.random.key(seed), 12)
    return {
        "tokens": noise_with(key_list[0], (TOKENS, D), 1.0, 6.0, ((0, 32),), (0, 1, 32, 2.75)),
        "in_weight": gaussian(key_list[1], (D, PROJ), D ** -0.5, 0.1875, ((0, 32),)),
        "out_weight": gaussian(key_list[2], (INNER, D), INNER ** -0.5, 0.125, ((1, 32),)),
        "conv_weight": gaussian(key_list[3], (KCONV, CONVDIM), KCONV ** -0.5, 3.0, ((1, 32),)),
        "conv_bias": jnp.clip(jax.random.uniform(key_list[4], (CONVDIM,), jnp.float32, -0.5, 0.5) * levels(key_list[4], (CONVDIM,), ((0, 32),), -0.4, 0.0), -0.5, 0.5).astype(jnp.bfloat16),
        "norm_gain": jnp.clip(1.0 + 0.1 * jax.random.normal(key_list[5], (D,), jnp.float32), 0.5, 1.5).astype(jnp.bfloat16),
        "gate_gain": jnp.clip(1.0 + 0.1 * jax.random.normal(key_list[6], (INNER,), jnp.float32), 0.5, 1.5).astype(jnp.bfloat16),
        "decay_log": jnp.clip(2.77 * jax.random.uniform(key_list[7], (HEADS,), jnp.float32) ** levels(key_list[7], (HEADS,), ((0, 4),), -0.2, 0.2), 0.0, 2.77),
        "step_bias": jnp.clip(-6.5 + 4.0 * jax.random.uniform(key_list[8], (HEADS,), jnp.float32) ** levels(key_list[8], (HEADS,), ((0, 4),), -0.2, 0.2), -6.5, -2.5),
        "skip_scale": jnp.clip(0.5 + 1.0 * jax.random.uniform(key_list[9], (HEADS,), jnp.float32) ** levels(key_list[9], (HEADS,), ((0, 4),), -0.2, 0.2), 0.5, 1.5),
        "cotangent": noise_with(key_list[10], (TOKENS, D), 1.0, 6.0, ((0, 32),), (0, 1, 32, 2.75)),
    }


EPSILON = 1e-05
precise = lax.Precision.HIGHEST

@jax.custom_vjp
def low(v):
    return lax.optimization_barrier(v.astype(jnp.bfloat16)).astype(jnp.float32)

@jax.custom_vjp
def low_back(v):
    return v

def low_keep(v):
    return (low(v), None)

def low_pass(kept, grad):
    return (grad,)

def back_keep(v):
    return (v, None)

def back_low(kept, grad):
    return (low(grad),)
low.defvjp(low_keep, low_pass)
low_back.defvjp(back_keep, back_low)

def forward(tokens, in_weight, out_weight, conv_weight, conv_bias, norm_gain, gate_gain, decay_log, step_bias, skip_scale):
    seq_count = tokens.shape[0]
    groups = SEQ_LEN // GROUP
    norm_scale = lax.rsqrt(lax.optimization_barrier(jnp.mean(tokens * tokens, axis=-1, keepdims=True)) + EPSILON)
    normed = low(tokens * norm_scale * norm_gain)
    projected = low_back(jnp.einsum('gld,de->gle', normed, in_weight, precision=precise))
    gate_in = projected[..., :INNER]
    conv_in = projected[..., INNER:INNER + CONVDIM]
    step_raw = projected[..., INNER + CONVDIM:]
    padded = jnp.pad(conv_in, ((0, 0), (KCONV - 1, 0), (0, 0)))
    pre_act = conv_bias + sum((conv_weight[conv_tap] * padded[:, conv_tap:conv_tap + SEQ_LEN] for conv_tap in range(KCONV)))
    active = jax.nn.silu(pre_act)
    values = active[..., :INNER]
    values_low = low(values).reshape(seq_count, groups, GROUP, HEADS, HEADDIM)
    b_low = low(active[..., INNER:INNER + STATE]).reshape(seq_count, groups, GROUP, STATE)
    c_low = low(active[..., INNER + STATE:]).reshape(seq_count, groups, GROUP, STATE)
    step_size = jax.nn.softplus(step_raw + step_bias)
    decay_rate = -jnp.exp(decay_log)
    step_heads = jnp.moveaxis(step_size.reshape(seq_count, groups, GROUP, HEADS), 3, 2)
    cumulated = jnp.cumsum(step_heads * decay_rate[:, None], axis=-1)
    row_ids = lax.broadcasted_iota(jnp.int32, (GROUP, GROUP), 0)
    col_ids = lax.broadcasted_iota(jnp.int32, (GROUP, GROUP), 1)
    causal = row_ids >= col_ids
    differ = cumulated[..., :, None] - cumulated[..., None, :]
    decay_table = jnp.where(causal, jnp.exp(jnp.where(causal, differ, 0.0)), 0.0)
    gram_matrix = low_back(jnp.einsum('gcqn,gcsn->gcqs', c_low, b_low, precision=precise))
    mixing = low(gram_matrix[:, :, None] * decay_table * step_heads[..., None, :])
    intra_out = jnp.einsum('gchqs,gcshp->gcqhp', mixing, values_low, precision=precise)
    last_cum = cumulated[..., -1:]
    weight_s = jnp.exp(last_cum - cumulated) * step_heads
    scaled_b = low(weight_s[..., None] * b_low[:, :, None])
    group_state = low_back(jnp.einsum('gchsn,gcshp->gchnp', scaled_b, values_low, precision=precise))
    group_decay = jnp.exp(last_cum[..., 0])
    carried = jnp.zeros((seq_count, HEADS, STATE, HEADDIM), jnp.float32)
    entering = []
    for group_index in range(groups):
        entering.append(carried)
        carried = group_decay[:, group_index, :, None, None] * carried + group_state[:, group_index]
    entering_low = low(jnp.stack(entering, axis=1))
    inter_raw = low_back(jnp.einsum('gcqn,gchnp->gcqhp', c_low, entering_low, precision=precise))
    inter_out = jnp.exp(jnp.moveaxis(cumulated, 2, 3))[..., None] * inter_raw
    ssm_out = (intra_out + inter_out).reshape(seq_count, SEQ_LEN, HEADS, HEADDIM) + skip_scale[:, None] * values.reshape(seq_count, SEQ_LEN, HEADS, HEADDIM)
    ssm_out = low_back(ssm_out.reshape(seq_count, SEQ_LEN, INNER))
    gated_out = ssm_out * jax.nn.silu(gate_in)
    gate_scale = lax.rsqrt(lax.optimization_barrier(jnp.mean(gated_out * gated_out, axis=-1, keepdims=True)) + EPSILON)
    mixed_low = low(gated_out * gate_scale * gate_gain)
    return tokens + jnp.einsum('gli,id->gld', mixed_low, out_weight, precision=precise)

def reference(tokens, in_weight, out_weight, conv_weight, conv_bias, norm_gain, gate_gain, decay_log, step_bias, skip_scale, cotangent):
    params = tuple((param.astype(jnp.float32) for param in (in_weight, out_weight, conv_weight, conv_bias, norm_gain, gate_gain, decay_log, step_bias, skip_scale)))
    block_count = TOKENS // SEQ_LEN // 2
    token_blocks = tokens.astype(jnp.float32).reshape(block_count, 2, SEQ_LEN, D)
    cot_blocks = cotangent.astype(jnp.float32).reshape(block_count, 2, SEQ_LEN, D)

    def one_block(running, block_pair):
        token_block, cot_block = block_pair
        result, pullback = jax.vjp(forward, token_block, *params)
        gradients = pullback(cot_block)
        running = tuple((earlier + addend for earlier, addend in zip(running, gradients[1:])))
        return (running, (result.astype(jnp.bfloat16), gradients[0].astype(jnp.bfloat16)))
    zeros = tuple((jnp.zeros_like(param) for param in params))
    running, (results, token_grads) = lax.scan(one_block, zeros, (token_blocks, cot_blocks))
    return (results.reshape(TOKENS, D), token_grads.reshape(TOKENS, D), running[0], running[1], running[2], running[3], running[4], running[5], running[6], running[7], running[8])
```

```python
import jax
import jax.numpy as jnp
from jax import lax
from jax.experimental import pallas as pl
from jax.experimental.pallas import tpu as pltpu
from jax.sharding import PartitionSpec as P

HEADS = 32
HEADDIM = 64
STATE = 128
KCONV = 4
GROUP = 256
SEQ_LEN = 1024
GROUPS = SEQ_LEN // GROUP
INNER = 2048
CONVDIM = 2304
PAIR = 2 * HEADDIM
EPSILON = 1e-05
AXES = ("dp", "fsdp")
f32 = jnp.float32
bf16 = jnp.bfloat16


def silu_slope(pre_act):
    logistic = jax.nn.sigmoid(pre_act)
    return logistic * (1.0 + pre_act * (1.0 - logistic))


def mm(a, b):
    return lax.dot_general(a, b, (((1,), (0,)), ((), ())), preferred_element_type=f32)


def mm_nt(a, b):
    return lax.dot_general(a, b, (((1,), (1,)), ((), ())), preferred_element_type=f32)


def mm_tn(a, b):
    return lax.dot_general(a, b, (((0,), (0,)), ((), ())), preferred_element_type=f32)


def causal_mask():
    rows = lax.broadcasted_iota(jnp.int32, (GROUP, GROUP), 0)
    return rows >= lax.broadcasted_iota(jnp.int32, (GROUP, GROUP), 1)


def scan_kernel(act_ref, cum_ref, step_ref, cum_t_ref, step_t_ref, skip_ref, y_ref, ent_ref, state):
    @pl.when(pl.program_id(0) % GROUPS == 0)
    def _():
        state[...] = jnp.zeros_like(state)

    b_low = act_ref[:, INNER : INNER + STATE]
    c_low = act_ref[:, INNER + STATE :]
    gram = jnp.where(causal_mask(), mm_nt(c_low, b_low), 0.0)
    cum = cum_ref[...]
    last = cum_ref[GROUP - 1 : GROUP, :]
    growth = jnp.exp(cum)
    weight = jnp.exp(last - cum) * step_ref[...]
    decay = jnp.exp(last)
    first = lax.broadcasted_iota(jnp.int32, (GROUP, PAIR), 1) < HEADDIM
    for pair in range(HEADS // 2):
        at = slice(pair * PAIR, (pair + 1) * PAIR)
        vals = act_ref[:, at]
        low, high = 2 * pair, 2 * pair + 1
        parts = []
        for head in (low, high):
            differ = cum[:, head : head + 1] - cum_t_ref[0, head : head + 1, :]
            table = jnp.exp(jnp.minimum(differ, 0.0))
            mixing = (gram * table * step_t_ref[0, head : head + 1, :]).astype(bf16)
            parts.append(mm(mixing, vals))

        def spread(cols):
            lanes = first[: cols.shape[0]]
            return jnp.where(lanes, cols[:, low : low + 1], cols[:, high : high + 1])

        carried = state[:, at]
        ent = carried.astype(bf16)
        ent_ref[0, :, at] = ent
        wide = vals.astype(f32)
        y_ref[:, at] = (
            jnp.where(first, parts[0], parts[1])
            + spread(growth) * mm(c_low, ent)
            + skip_ref[:, at] * wide
        )
        weighted = (spread(weight) * wide).astype(bf16)
        state[:, at] = spread(decay) * carried + mm_tn(b_low, weighted)


def scan_back_kernel(
    dy_ref, act_ref, ent_ref, cum_ref, step_ref, cum_t_ref, step_t_ref, skip_ref,
    dact_ref, row_ref, wg_ref, col_ref, stat_ref, carried_ref, gram_acc, b_acc, c_acc,
):
    @pl.when(pl.program_id(0) % GROUPS == 0)
    def _():
        carried_ref[...] = jnp.zeros_like(carried_ref)

    b_low = act_ref[:, INNER : INNER + STATE]
    c_low = act_ref[:, INNER + STATE :]
    causal = causal_mask()
    gram = jnp.where(causal, mm_nt(c_low, b_low), 0.0)
    gram_acc[...] = jnp.zeros_like(gram_acc)
    b_acc[...] = jnp.zeros_like(b_acc)
    c_acc[...] = jnp.zeros_like(c_acc)
    cum = cum_ref[...]
    last = cum_ref[GROUP - 1 : GROUP, :]
    growth = jnp.exp(cum)
    weight = jnp.exp(last - cum) * step_ref[...]
    decay = jnp.exp(last)
    first = lax.broadcasted_iota(jnp.int32, (GROUP, PAIR), 1) < HEADDIM
    for pair in range(HEADS // 2):
        at = slice(pair * PAIR, (pair + 1) * PAIR)
        vals = act_ref[:, at]
        dy = dy_ref[:, at]
        low, high = 2 * pair, 2 * pair + 1
        wide = vals.astype(f32)
        dy_wide = dy.astype(f32)
        parts = []
        row_sums = []
        for head in (low, high):
            differ = cum[:, head : head + 1] - cum_t_ref[0, head : head + 1, :]
            table = jnp.exp(jnp.minimum(differ, 0.0))
            steps = step_t_ref[0, head : head + 1, :]
            own = first if head == low else jnp.logical_not(first)
            mixing_grad = mm_nt(jnp.where(own, dy_wide, 0.0).astype(bf16), vals)
            shaded = gram * table
            mixing = shaded * steps
            col_ref[0, head : head + 1, :] = jnp.sum(mixing_grad * shaded, axis=0, keepdims=True)
            row_sums.append(jnp.sum(mixing_grad * mixing, axis=1, keepdims=True))
            gram_acc[...] += mixing_grad * (table * steps)
            parts.append(mm_tn(mixing.astype(bf16), dy))

        def spread(cols):
            lanes = first[: cols.shape[0]]
            return jnp.where(lanes, cols[:, low : low + 1], cols[:, high : high + 1])

        ent = ent_ref[0, :, at]
        carried = carried_ref[:, at]
        state_grad = carried.astype(bf16)
        from_state = mm(b_low, state_grad)
        weights = spread(weight)
        dact_ref[:, at] = (
            jnp.where(first, parts[0], parts[1]) + weights * from_state + skip_ref[:, at] * dy_wide
        )
        raw = spread(growth) * dy_wide
        raw_low = raw.astype(bf16)
        inter = raw * mm(c_low, ent)
        state_term = wide * from_state
        for head, sums, own in ((low, row_sums[0], first), (high, row_sums[1], jnp.logical_not(first))):
            row_ref[:, head : head + 1] = sums + jnp.sum(
                jnp.where(own, inter, 0.0), axis=1, keepdims=True
            )
            wg_ref[:, head : head + 1] = jnp.sum(
                jnp.where(own, state_term, 0.0), axis=1, keepdims=True
            )
        stat_ref[0, 0:1, at] = jnp.sum(carried * ent.astype(f32), axis=0, keepdims=True)
        stat_ref[0, 1:2, at] = jnp.sum(dy_wide * wide, axis=0, keepdims=True)
        carried_ref[:, at] = mm_tn(c_low, raw_low) + spread(decay) * carried
        c_acc[...] += mm_nt(raw_low, ent)
        b_acc[...] += mm_nt((weights * wide).astype(bf16), state_grad)
    stat_ref[0, 2:8, :] = jnp.zeros((6, INNER), f32)
    gram_grad = jnp.where(causal, gram_acc[...], 0.0).astype(bf16)
    dact_ref[:, INNER : INNER + STATE] = b_acc[...] + mm_tn(gram_grad, c_low)
    dact_ref[:, INNER + STATE :] = c_acc[...] + mm(gram_grad, b_low)


def specs_for(order):
    def rows(width):
        return pl.BlockSpec((GROUP, width), lambda g: (order(g), 0))

    def cube(height, width):
        return pl.BlockSpec((1, height, width), lambda g: (order(g), 0, 0))

    return rows, cube, pl.BlockSpec((1, INNER), lambda g: (0, 0))


def scan_forward(act, cum, step, cum_t, step_t, skip):
    count = act.shape[0] // GROUP
    rows, cube, whole = specs_for(lambda g: g)
    return pl.pallas_call(
        scan_kernel,
        grid=(count,),
        in_specs=[rows(CONVDIM), rows(HEADS), rows(HEADS), cube(HEADS, GROUP), cube(HEADS, GROUP), whole],
        out_specs=[rows(INNER), cube(STATE, INNER)],
        out_shape=[
            jax.ShapeDtypeStruct((act.shape[0], INNER), f32),
            jax.ShapeDtypeStruct((count, STATE, INNER), bf16),
        ],
        scratch_shapes=[pltpu.VMEM((STATE, INNER), f32)],
        compiler_params=pltpu.CompilerParams(
            dimension_semantics=("arbitrary",), vmem_limit_bytes=40 * 2**20
        ),
        cost_estimate=pl.CostEstimate(
            flops=count * 2 * 10**9, bytes_accessed=act.shape[0] * 15000, transcendentals=count * 2**21
        ),
    )(act, cum, step, cum_t, step_t, skip)


def scan_backward(dy, act, ent, cum, step, cum_t, step_t, skip):
    count = act.shape[0] // GROUP
    rows, cube, whole = specs_for(lambda g: g // GROUPS * GROUPS + GROUPS - 1 - g % GROUPS)
    return pl.pallas_call(
        scan_back_kernel,
        grid=(count,),
        in_specs=[
            rows(INNER), rows(CONVDIM), cube(STATE, INNER), rows(HEADS), rows(HEADS),
            cube(HEADS, GROUP), cube(HEADS, GROUP), whole,
        ],
        out_specs=[rows(CONVDIM), rows(HEADS), rows(HEADS), cube(HEADS, GROUP), cube(8, INNER)],
        out_shape=[
            jax.ShapeDtypeStruct((act.shape[0], CONVDIM), f32),
            jax.ShapeDtypeStruct((act.shape[0], HEADS), f32),
            jax.ShapeDtypeStruct((act.shape[0], HEADS), f32),
            jax.ShapeDtypeStruct((count, HEADS, GROUP), f32),
            jax.ShapeDtypeStruct((count, 8, INNER), f32),
        ],
        scratch_shapes=[
            pltpu.VMEM((STATE, INNER), f32),
            pltpu.VMEM((GROUP, GROUP), f32),
            pltpu.VMEM((GROUP, STATE), f32),
            pltpu.VMEM((GROUP, STATE), f32),
        ],
        compiler_params=pltpu.CompilerParams(
            dimension_semantics=("arbitrary",), vmem_limit_bytes=40 * 2**20
        ),
        cost_estimate=pl.CostEstimate(
            flops=count * 4 * 10**9, bytes_accessed=act.shape[0] * 20000, transcendentals=count * 2**21
        ),
    )(dy, act, ent, cum, step, cum_t, step_t, skip)


def group_cumsum(a, suffix):
    tri = causal_mask().astype(f32)
    return jnp.einsum(
        "rt,grh->gth" if suffix else "tr,grh->gth",
        tri, a.reshape(-1, GROUP, HEADS), precision=lax.Precision.HIGHEST,
    ).reshape(-1, HEADS)


def gather_weights(in_weight, conv_weight, conv_bias, norm_gain, gate_gain):
    rows, cols = in_weight.shape
    spare = -cols % 128
    small = jnp.concatenate([conv_weight.reshape(-1), conv_bias, norm_gain, gate_gain])
    side = jnp.pad(small, (0, rows * spare - small.shape[0])).reshape(rows, spare)
    whole = lax.all_gather(
        jnp.concatenate([in_weight, side], axis=1), AXES, axis=0, tiled=True
    )
    side = whole[:, cols:].reshape(-1, rows * spare)
    devices = side.shape[0]
    start = 0
    pieces = []
    for size in (conv_weight.size, conv_bias.size, norm_gain.size, gate_gain.size):
        pieces.append(side[:, start : start + size])
        start += size
    taps = pieces[0].reshape(devices, KCONV, -1).swapaxes(0, 1).reshape(KCONV, -1)
    return whole, taps, pieces[1].reshape(-1), pieces[2].reshape(-1), pieces[3].reshape(-1)


def on_device(
    tokens, in_weight, out_weight, conv_weight, conv_bias, norm_gain, gate_gain,
    decay_log, step_bias, skip_scale, cotangent,
):
    whole, taps, bias_all, norm_all, gate_all = gather_weights(
        in_weight, conv_weight, conv_bias, norm_gain, gate_gain
    )
    out_all = lax.all_gather(out_weight, AXES, axis=1, tiled=True)
    head_all = lax.all_gather(
        jnp.stack([decay_log, step_bias, skip_scale]), "fsdp", axis=1, tiled=True
    )
    decay_rate = -jnp.exp(head_all[0])
    skip_row = jnp.repeat(head_all[2], HEADDIM)[None]
    seq_count = tokens.shape[0] // SEQ_LEN
    count = tokens.shape[0] // GROUP
    taps = taps.astype(f32)
    norm_all = norm_all.astype(f32)
    gate_all = gate_all.astype(f32)

    inputs = tokens.astype(f32)
    norm_scale = lax.rsqrt(jnp.mean(inputs * inputs, axis=-1, keepdims=True) + EPSILON)
    normed = (inputs * norm_scale * norm_all).astype(bf16)
    w_gate = whole[:, :INNER]
    w_conv = whole[:, INNER : INNER + CONVDIM]
    w_step = whole[:, INNER + CONVDIM : INNER + CONVDIM + HEADS]
    conv_in = mm(normed, w_conv).reshape(seq_count, SEQ_LEN, CONVDIM)
    step_raw = mm(normed, w_step)
    gate_in = mm(normed, w_gate)
    padded = jnp.pad(conv_in, ((0, 0), (KCONV - 1, 0), (0, 0)))
    pre_act = bias_all.astype(f32) + sum(taps[k] * padded[:, k : k + SEQ_LEN] for k in range(KCONV))
    act = jax.nn.silu(pre_act).astype(bf16).reshape(-1, CONVDIM)
    step = jax.nn.softplus(step_raw + head_all[1])
    cum = group_cumsum(step * decay_rate, False)
    cum_t = cum.reshape(count, GROUP, HEADS).swapaxes(1, 2)
    step_t = step.reshape(count, GROUP, HEADS).swapaxes(1, 2)
    ssm_out, ent = scan_forward(act, cum, step, cum_t, step_t, skip_row)

    silu_gate = jax.nn.silu(gate_in)
    gated_out = ssm_out * silu_gate
    gate_scale = lax.rsqrt(jnp.mean(gated_out * gated_out, axis=-1, keepdims=True) + EPSILON)
    mixed_low = (gated_out * gate_scale * gate_all).astype(bf16)
    output = (inputs + mm(mixed_low, out_all)).astype(bf16)

    out_share = lax.psum_scatter(
        mm_tn(mixed_low, cotangent).astype(bf16), AXES, scatter_dimension=1, tiled=True
    ).astype(f32)
    mixed_grad = mm_nt(cotangent, out_all)
    gate_gain_grad = jnp.sum(mixed_grad * gated_out * gate_scale, axis=0)
    scaled_in = mixed_grad * gate_all
    gated_grad = gate_scale * (
        scaled_in
        - gated_out * gate_scale * gate_scale
        * jnp.mean(scaled_in * gated_out, axis=-1, keepdims=True)
    )
    ssm_grad = (gated_grad * silu_gate).astype(bf16)
    gate_grad = (gated_grad * ssm_out * silu_slope(gate_in)).astype(bf16)
    gate_cols = lax.psum_scatter(
        mm_tn(normed, gate_grad).astype(bf16), AXES, scatter_dimension=0, tiled=True
    )

    dact, row, weight_grad, col_t, stats = scan_backward(
        ssm_grad, act, ent, cum, step, cum_t, step_t, skip_row
    )
    col = col_t.swapaxes(1, 2).reshape(-1, HEADS)
    grouped = (count, GROUP, HEADS)
    last = cum.reshape(grouped)[:, -1:]
    fading = jnp.exp(last - cum.reshape(grouped)).reshape(-1, HEADS)
    weight_term = weight_grad * fading * step
    decay_grad = jnp.sum(stats[:, 0].reshape(count, HEADS, HEADDIM), axis=-1)
    last_grad = jnp.sum(weight_term.reshape(grouped), axis=1) + decay_grad * jnp.exp(last[:, 0])
    skip_grad = jnp.sum(stats[:, 1].reshape(count, HEADS, HEADDIM), axis=(0, 2))
    cum_grad = row - step * col - weight_term
    rate_grad = (
        group_cumsum(cum_grad, True).reshape(grouped) + last_grad[:, None]
    ).reshape(-1, HEADS)
    step_grad = col + weight_grad * fading + rate_grad * decay_rate
    decay_log_grad = jnp.sum(rate_grad * step, axis=0) * decay_rate
    step_raw_grad = step_grad * jax.nn.sigmoid(step_raw + head_all[1])
    step_bias_grad = jnp.sum(step_raw_grad, axis=0)

    pre_grad = dact.reshape(seq_count, SEQ_LEN, CONVDIM) * silu_slope(pre_act)
    conv_bias_grad = jnp.sum(pre_grad, axis=(0, 1))
    conv_weight_grad = jnp.stack(
        [jnp.sum(pre_grad * padded[:, k : k + SEQ_LEN], axis=(0, 1)) for k in range(KCONV)]
    )
    grad_padded = jnp.pad(pre_grad, ((0, 0), (0, KCONV - 1), (0, 0)))
    conv_in_grad = sum(
        taps[k] * grad_padded[:, KCONV - 1 - k : KCONV - 1 - k + SEQ_LEN] for k in range(KCONV)
    )
    conv_in_grad = conv_in_grad.astype(bf16).reshape(-1, CONVDIM)
    step_low = step_raw_grad.astype(bf16)
    late = jnp.concatenate([mm_tn(normed, conv_in_grad), mm_tn(normed, step_low)], axis=1)
    late_cols = lax.psum_scatter(late.astype(bf16), AXES, scatter_dimension=0, tiled=True)
    in_share = jnp.concatenate([gate_cols, late_cols], axis=1).astype(f32)
    normed_grad = (
        mm_nt(gate_grad, w_gate) + mm_nt(conv_in_grad, w_conv) + mm_nt(step_low, w_step)
    )
    norm_share = jnp.sum(in_share * in_weight.astype(f32), axis=1) / norm_gain.astype(f32)
    scaled_in = normed_grad * norm_all
    token_grad = norm_scale * (
        scaled_in
        - inputs * norm_scale * norm_scale * jnp.mean(scaled_in * inputs, axis=-1, keepdims=True)
    ) + cotangent.astype(f32)

    totals = lax.psum(
        jnp.concatenate(
            [conv_weight_grad.reshape(-1), conv_bias_grad, gate_gain_grad,
             decay_log_grad, step_bias_grad, skip_grad]
        ),
        AXES,
    )
    me = lax.axis_index("dp") * lax.axis_size("fsdp") + lax.axis_index("fsdp")
    conv_total = totals[: KCONV * CONVDIM].reshape(KCONV, CONVDIM)
    start = KCONV * CONVDIM
    width = conv_weight.shape[1]
    conv_weight_share = lax.dynamic_slice_in_dim(conv_total, me * width, width, axis=1)
    conv_bias_share = lax.dynamic_slice_in_dim(totals, start + me * width, width)
    start += CONVDIM
    wide = gate_gain.shape[0]
    gate_share = lax.dynamic_slice_in_dim(totals, start + me * wide, wide)
    start += INNER
    share = decay_log.shape[0]
    own = lax.axis_index("fsdp") * share
    heads = [
        lax.dynamic_slice_in_dim(totals, start + i * HEADS + own, share) for i in range(3)
    ]
    return (
        output, token_grad.astype(bf16), in_share, out_share, conv_weight_share,
        conv_bias_share, norm_share, gate_share, *heads,
    )


def solution(mesh):
    return jax.shard_map(
        on_device,
        mesh=mesh,
        in_specs=(
            P(("dp", "fsdp"), None),
            P(("dp", "fsdp"), None),
            P(None, ("dp", "fsdp")),
            P(None, ("dp", "fsdp")),
            P(("dp", "fsdp")),
            P(("dp", "fsdp")),
            P(("dp", "fsdp")),
            P("fsdp"),
            P("fsdp"),
            P("fsdp"),
            P(("dp", "fsdp"), None),
        ),
        out_specs=(
            P(("dp", "fsdp"), None),
            P(("dp", "fsdp"), None),
            P(("dp", "fsdp"), None),
            P(None, ("dp", "fsdp")),
            P(None, ("dp", "fsdp")),
            P(("dp", "fsdp")),
            P(("dp", "fsdp")),
            P(("dp", "fsdp")),
            P("fsdp"),
            P("fsdp"),
            P("fsdp"),
        ),
        check_vma=False,
    )
```

```python
import jax
import jax.numpy as jnp
from jax import lax
from jax.experimental import pallas as pl
from jax.experimental.pallas import tpu as pltpu
from jax.sharding import PartitionSpec as P

HEADS = 32
HEADDIM = 64
STATE = 128
KCONV = 4
GROUP = 256
SEQ_LEN = 1024
GROUPS = SEQ_LEN // GROUP
INNER = 2048
CONVDIM = 2304
PAIR = 2 * HEADDIM
EPSILON = 1e-05
AXES = ("dp", "fsdp")
f32 = jnp.float32
bf16 = jnp.bfloat16


def silu_slope(pre_act):
    logistic = jax.nn.sigmoid(pre_act)
    return logistic * (1.0 + pre_act * (1.0 - logistic))


def mm(a, b):
    return lax.dot_general(a, b, (((1,), (0,)), ((), ())), preferred_element_type=f32)


def mm_nt(a, b):
    return lax.dot_general(a, b, (((1,), (1,)), ((), ())), preferred_element_type=f32)


def mm_tn(a, b):
    return lax.dot_general(a, b, (((0,), (0,)), ((), ())), preferred_element_type=f32)


def causal_mask():
    rows = lax.broadcasted_iota(jnp.int32, (GROUP, GROUP), 0)
    return rows >= lax.broadcasted_iota(jnp.int32, (GROUP, GROUP), 1)


def scan_kernel(act_ref, cum_ref, step_ref, cum_t_ref, step_t_ref, skip_ref, y_ref, ent_ref, state):
    @pl.when(pl.program_id(0) % GROUPS == 0)
    def _():
        state[...] = jnp.zeros_like(state)

    b_low = act_ref[:, INNER : INNER + STATE]
    c_low = act_ref[:, INNER + STATE :]
    gram = jnp.where(causal_mask(), mm_nt(c_low, b_low), 0.0)
    cum = cum_ref[...]
    last = cum_ref[GROUP - 1 : GROUP, :]
    growth = jnp.exp(cum)
    weight = jnp.exp(last - cum) * step_ref[...]
    decay = jnp.exp(last)
    first = lax.broadcasted_iota(jnp.int32, (GROUP, PAIR), 1) < HEADDIM
    for pair in range(HEADS // 2):
        at = slice(pair * PAIR, (pair + 1) * PAIR)
        vals = act_ref[:, at]
        low, high = 2 * pair, 2 * pair + 1
        parts = []
        for head in (low, high):
            differ = cum[:, head : head + 1] - cum_t_ref[0, head : head + 1, :]
            table = jnp.exp(jnp.minimum(differ, 0.0))
            mixing = (gram * table * step_t_ref[0, head : head + 1, :]).astype(bf16)
            parts.append(mm(mixing, vals))

        def spread(cols):
            lanes = first[: cols.shape[0]]
            return jnp.where(lanes, cols[:, low : low + 1], cols[:, high : high + 1])

        carried = state[:, at]
        ent = carried.astype(bf16)
        ent_ref[0, :, at] = ent
        wide = vals.astype(f32)
        y_ref[:, at] = (
            jnp.where(first, parts[0], parts[1])
            + spread(growth) * mm(c_low, ent)
            + skip_ref[:, at] * wide
        )
        weighted = (spread(weight) * wide).astype(bf16)
        state[:, at] = spread(decay) * carried + mm_tn(b_low, weighted)


def scan_back_kernel(
    dy_ref, act_ref, ent_ref, cum_ref, step_ref, cum_t_ref, step_t_ref, skip_ref,
    dact_ref, row_ref, wg_ref, col_ref, stat_ref, carried_ref, gram_acc, b_acc, c_acc,
):
    @pl.when(pl.program_id(0) % GROUPS == 0)
    def _():
        carried_ref[...] = jnp.zeros_like(carried_ref)

    b_low = act_ref[:, INNER : INNER + STATE]
    c_low = act_ref[:, INNER + STATE :]
    causal = causal_mask()
    gram = jnp.where(causal, mm_nt(c_low, b_low), 0.0)
    gram_acc[...] = jnp.zeros_like(gram_acc)
    b_acc[...] = jnp.zeros_like(b_acc)
    c_acc[...] = jnp.zeros_like(c_acc)
    cum = cum_ref[...]
    last = cum_ref[GROUP - 1 : GROUP, :]
    growth = jnp.exp(cum)
    weight = jnp.exp(last - cum) * step_ref[...]
    decay = jnp.exp(last)
    first = lax.broadcasted_iota(jnp.int32, (GROUP, PAIR), 1) < HEADDIM
    for pair in range(HEADS // 2):
        at = slice(pair * PAIR, (pair + 1) * PAIR)
        vals = act_ref[:, at]
        dy = dy_ref[:, at]
        low, high = 2 * pair, 2 * pair + 1
        wide = vals.astype(f32)
        dy_wide = dy.astype(f32)
        parts = []
        row_sums = []
        for head in (low, high):
            differ = cum[:, head : head + 1] - cum_t_ref[0, head : head + 1, :]
            table = jnp.exp(jnp.minimum(differ, 0.0))
            steps = step_t_ref[0, head : head + 1, :]
            own = first if head == low else jnp.logical_not(first)
            mixing_grad = mm_nt(jnp.where(own, dy_wide, 0.0).astype(bf16), vals)
            shaded = gram * table
            mixing = shaded * steps
            col_ref[0, head : head + 1, :] = jnp.sum(mixing_grad * shaded, axis=0, keepdims=True)
            row_sums.append(jnp.sum(mixing_grad * mixing, axis=1, keepdims=True))
            gram_acc[...] += mixing_grad * (table * steps)
            parts.append(mm_tn(mixing.astype(bf16), dy))

        def spread(cols):
            lanes = first[: cols.shape[0]]
            return jnp.where(lanes, cols[:, low : low + 1], cols[:, high : high + 1])

        ent = ent_ref[0, :, at]
        carried = carried_ref[:, at]
        state_grad = carried.astype(bf16)
        from_state = mm(b_low, state_grad)
        weights = spread(weight)
        dact_ref[:, at] = (
            jnp.where(first, parts[0], parts[1]) + weights * from_state + skip_ref[:, at] * dy_wide
        )
        raw = spread(growth) * dy_wide
        raw_low = raw.astype(bf16)
        inter = raw * mm(c_low, ent)
        state_term = wide * from_state
        for head, sums, own in ((low, row_sums[0], first), (high, row_sums[1], jnp.logical_not(first))):
            row_ref[:, head : head + 1] = sums + jnp.sum(
                jnp.where(own, inter, 0.0), axis=1, keepdims=True
            )
            wg_ref[:, head : head + 1] = jnp.sum(
                jnp.where(own, state_term, 0.0), axis=1, keepdims=True
            )
        stat_ref[0, 0:1, at] = jnp.sum(carried * ent.astype(f32), axis=0, keepdims=True)
        stat_ref[0, 1:2, at] = jnp.sum(dy_wide * wide, axis=0, keepdims=True)
        carried_ref[:, at] = mm_tn(c_low, raw_low) + spread(decay) * carried
        c_acc[...] += mm_nt(raw_low, ent)
        b_acc[...] += mm_nt((weights * wide).astype(bf16), state_grad)
    stat_ref[0, 2:8, :] = jnp.zeros((6, INNER), f32)
    gram_grad = jnp.where(causal, gram_acc[...], 0.0).astype(bf16)
    dact_ref[:, INNER : INNER + STATE] = b_acc[...] + mm_tn(gram_grad, c_low)
    dact_ref[:, INNER + STATE :] = c_acc[...] + mm(gram_grad, b_low)


def specs_for(order):
    def rows(width):
        return pl.BlockSpec((GROUP, width), lambda g: (order(g), 0))

    def cube(height, width):
        return pl.BlockSpec((1, height, width), lambda g: (order(g), 0, 0))

    return rows, cube, pl.BlockSpec((1, INNER), lambda g: (0, 0))


def scan_forward(act, cum, step, cum_t, step_t, skip):
    count = act.shape[0] // GROUP
    rows, cube, whole = specs_for(lambda g: g)
    return pl.pallas_call(
        scan_kernel,
        grid=(count,),
        in_specs=[rows(CONVDIM), rows(HEADS), rows(HEADS), cube(HEADS, GROUP), cube(HEADS, GROUP), whole],
        out_specs=[rows(INNER), cube(STATE, INNER)],
        out_shape=[
            jax.ShapeDtypeStruct((act.shape[0], INNER), f32),
            jax.ShapeDtypeStruct((count, STATE, INNER), bf16),
        ],
        scratch_shapes=[pltpu.VMEM((STATE, INNER), f32)],
        compiler_params=pltpu.CompilerParams(
            dimension_semantics=("arbitrary",), vmem_limit_bytes=40 * 2**20
        ),
        cost_estimate=pl.CostEstimate(
            flops=count * 2 * 10**9, bytes_accessed=act.shape[0] * 15000, transcendentals=count * 2**21
        ),
    )(act, cum, step, cum_t, step_t, skip)


def scan_backward(dy, act, ent, cum, step, cum_t, step_t, skip):
    count = act.shape[0] // GROUP
    rows, cube, whole = specs_for(lambda g: g // GROUPS * GROUPS + GROUPS - 1 - g % GROUPS)
    return pl.pallas_call(
        scan_back_kernel,
        grid=(count,),
        in_specs=[
            rows(INNER), rows(CONVDIM), cube(STATE, INNER), rows(HEADS), rows(HEADS),
            cube(HEADS, GROUP), cube(HEADS, GROUP), whole,
        ],
        out_specs=[rows(CONVDIM), rows(HEADS), rows(HEADS), cube(HEADS, GROUP), cube(8, INNER)],
        out_shape=[
            jax.ShapeDtypeStruct((act.shape[0], CONVDIM), f32),
            jax.ShapeDtypeStruct((act.shape[0], HEADS), f32),
            jax.ShapeDtypeStruct((act.shape[0], HEADS), f32),
            jax.ShapeDtypeStruct((count, HEADS, GROUP), f32),
            jax.ShapeDtypeStruct((count, 8, INNER), f32),
        ],
        scratch_shapes=[
            pltpu.VMEM((STATE, INNER), f32),
            pltpu.VMEM((GROUP, GROUP), f32),
            pltpu.VMEM((GROUP, STATE), f32),
            pltpu.VMEM((GROUP, STATE), f32),
        ],
        compiler_params=pltpu.CompilerParams(
            dimension_semantics=("arbitrary",), vmem_limit_bytes=40 * 2**20
        ),
        cost_estimate=pl.CostEstimate(
            flops=count * 4 * 10**9, bytes_accessed=act.shape[0] * 20000, transcendentals=count * 2**21
        ),
    )(dy, act, ent, cum, step, cum_t, step_t, skip)


def group_cumsum(a, suffix):
    tri = causal_mask().astype(f32)
    return jnp.einsum(
        "rt,grh->gth" if suffix else "tr,grh->gth",
        tri, a.reshape(-1, GROUP, HEADS), precision=lax.Precision.HIGHEST,
    ).reshape(-1, HEADS)


def gather_weights(in_weight, conv_weight, conv_bias, norm_gain, gate_gain):
    rows, cols = in_weight.shape
    spare = -cols % 128
    small = jnp.concatenate([conv_weight.reshape(-1), conv_bias, norm_gain, gate_gain])
    side = jnp.pad(small, (0, rows * spare - small.shape[0])).reshape(rows, spare)
    whole = lax.all_gather(
        jnp.concatenate([in_weight, side], axis=1), AXES, axis=0, tiled=True
    )
    side = whole[:, cols:].reshape(-1, rows * spare)
    devices = side.shape[0]
    start = 0
    pieces = []
    for size in (conv_weight.size, conv_bias.size, norm_gain.size, gate_gain.size):
        pieces.append(side[:, start : start + size])
        start += size
    taps = pieces[0].reshape(devices, KCONV, -1).swapaxes(0, 1).reshape(KCONV, -1)
    return whole, taps, pieces[1].reshape(-1), pieces[2].reshape(-1), pieces[3].reshape(-1)


def on_device(
    tokens, in_weight, out_weight, conv_weight, conv_bias, norm_gain, gate_gain,
    decay_log, step_bias, skip_scale, cotangent,
):
    whole, taps, bias_all, norm_all, gate_all = gather_weights(
        in_weight, conv_weight, conv_bias, norm_gain, gate_gain
    )
    whole, out_weight = lax.optimization_barrier((whole, out_weight))
    out_all = lax.all_gather(out_weight, AXES, axis=1, tiled=True)
    head_all = lax.all_gather(
        jnp.stack([decay_log, step_bias, skip_scale]), "fsdp", axis=1, tiled=True
    )
    decay_rate = -jnp.exp(head_all[0])
    skip_row = jnp.repeat(head_all[2], HEADDIM)[None]
    seq_count = tokens.shape[0] // SEQ_LEN
    count = tokens.shape[0] // GROUP
    taps = taps.astype(f32)
    norm_all = norm_all.astype(f32)
    gate_all = gate_all.astype(f32)

    inputs = tokens.astype(f32)
    norm_scale = lax.rsqrt(jnp.mean(inputs * inputs, axis=-1, keepdims=True) + EPSILON)
    normed = (inputs * norm_scale * norm_all).astype(bf16)
    w_gate = whole[:, :INNER]
    w_conv = whole[:, INNER : INNER + CONVDIM]
    w_step = whole[:, INNER + CONVDIM : INNER + CONVDIM + HEADS]
    conv_in = mm(normed, w_conv).reshape(seq_count, SEQ_LEN, CONVDIM)
    step_raw = mm(normed, w_step)
    gate_in = mm(normed, w_gate)
    padded = jnp.pad(conv_in, ((0, 0), (KCONV - 1, 0), (0, 0)))
    pre_act = bias_all.astype(f32) + sum(taps[k] * padded[:, k : k + SEQ_LEN] for k in range(KCONV))
    act = jax.nn.silu(pre_act).astype(bf16).reshape(-1, CONVDIM)
    step = jax.nn.softplus(step_raw + head_all[1])
    cum = group_cumsum(step * decay_rate, False)
    cum_t = cum.reshape(count, GROUP, HEADS).swapaxes(1, 2)
    step_t = step.reshape(count, GROUP, HEADS).swapaxes(1, 2)
    ssm_out, ent = scan_forward(act, cum, step, cum_t, step_t, skip_row)

    silu_gate = jax.nn.silu(gate_in)
    gated_out = ssm_out * silu_gate
    gate_scale = lax.rsqrt(jnp.mean(gated_out * gated_out, axis=-1, keepdims=True) + EPSILON)
    mixed_low = (gated_out * gate_scale * gate_all).astype(bf16)
    output = (inputs + mm(mixed_low, out_all)).astype(bf16)

    out_share = lax.psum_scatter(
        mm_tn(mixed_low, cotangent).astype(bf16), AXES, scatter_dimension=1, tiled=True
    ).astype(f32)
    mixed_grad = mm_nt(cotangent, out_all)
    gate_gain_grad = jnp.sum(mixed_grad * gated_out * gate_scale, axis=0)
    scaled_in = mixed_grad * gate_all
    gated_grad = gate_scale * (
        scaled_in
        - gated_out * gate_scale * gate_scale
        * jnp.mean(scaled_in * gated_out, axis=-1, keepdims=True)
    )
    ssm_grad = (gated_grad * silu_gate).astype(bf16)
    gate_grad = (gated_grad * ssm_out * silu_slope(gate_in)).astype(bf16)
    gate_cols = lax.psum_scatter(
        mm_tn(normed, gate_grad).astype(bf16), AXES, scatter_dimension=0, tiled=True
    )

    dact, row, weight_grad, col_t, stats = scan_backward(
        ssm_grad, act, ent, cum, step, cum_t, step_t, skip_row
    )
    col = col_t.swapaxes(1, 2).reshape(-1, HEADS)
    grouped = (count, GROUP, HEADS)
    last = cum.reshape(grouped)[:, -1:]
    fading = jnp.exp(last - cum.reshape(grouped)).reshape(-1, HEADS)
    weight_term = weight_grad * fading * step
    decay_grad = jnp.sum(stats[:, 0].reshape(count, HEADS, HEADDIM), axis=-1)
    last_grad = jnp.sum(weight_term.reshape(grouped), axis=1) + decay_grad * jnp.exp(last[:, 0])
    skip_grad = jnp.sum(stats[:, 1].reshape(count, HEADS, HEADDIM), axis=(0, 2))
    cum_grad = row - step * col - weight_term
    rate_grad = (
        group_cumsum(cum_grad, True).reshape(grouped) + last_grad[:, None]
    ).reshape(-1, HEADS)
    step_grad = col + weight_grad * fading + rate_grad * decay_rate
    decay_log_grad = jnp.sum(rate_grad * step, axis=0) * decay_rate
    step_raw_grad = step_grad * jax.nn.sigmoid(step_raw + head_all[1])
    step_bias_grad = jnp.sum(step_raw_grad, axis=0)

    pre_grad = dact.reshape(seq_count, SEQ_LEN, CONVDIM) * silu_slope(pre_act)
    conv_bias_grad = jnp.sum(pre_grad, axis=(0, 1))
    conv_weight_grad = jnp.stack(
        [jnp.sum(pre_grad * padded[:, k : k + SEQ_LEN], axis=(0, 1)) for k in range(KCONV)]
    )
    grad_padded = jnp.pad(pre_grad, ((0, 0), (0, KCONV - 1), (0, 0)))
    conv_in_grad = sum(
        taps[k] * grad_padded[:, KCONV - 1 - k : KCONV - 1 - k + SEQ_LEN] for k in range(KCONV)
    )
    conv_in_grad = conv_in_grad.astype(bf16).reshape(-1, CONVDIM)
    step_low = step_raw_grad.astype(bf16)
    late = jnp.concatenate([mm_tn(normed, conv_in_grad), mm_tn(normed, step_low)], axis=1)
    late_cols = lax.psum_scatter(late.astype(bf16), AXES, scatter_dimension=0, tiled=True)
    in_share = jnp.concatenate([gate_cols, late_cols], axis=1).astype(f32)
    normed_grad = (
        mm_nt(gate_grad, w_gate) + mm_nt(conv_in_grad, w_conv) + mm_nt(step_low, w_step)
    )
    norm_share = jnp.sum(in_share * in_weight.astype(f32), axis=1) / norm_gain.astype(f32)
    scaled_in = normed_grad * norm_all
    token_grad = norm_scale * (
        scaled_in
        - inputs * norm_scale * norm_scale * jnp.mean(scaled_in * inputs, axis=-1, keepdims=True)
    ) + cotangent.astype(f32)

    totals = lax.psum(
        jnp.concatenate(
            [conv_weight_grad.reshape(-1), conv_bias_grad, gate_gain_grad,
             decay_log_grad, step_bias_grad, skip_grad]
        ),
        AXES,
    )
    me = lax.axis_index("dp") * lax.axis_size("fsdp") + lax.axis_index("fsdp")
    conv_total = totals[: KCONV * CONVDIM].reshape(KCONV, CONVDIM)
    start = KCONV * CONVDIM
    width = conv_weight.shape[1]
    conv_weight_share = lax.dynamic_slice_in_dim(conv_total, me * width, width, axis=1)
    conv_bias_share = lax.dynamic_slice_in_dim(totals, start + me * width, width)
    start += CONVDIM
    wide = gate_gain.shape[0]
    gate_share = lax.dynamic_slice_in_dim(totals, start + me * wide, wide)
    start += INNER
    share = decay_log.shape[0]
    own = lax.axis_index("fsdp") * share
    heads = [
        lax.dynamic_slice_in_dim(totals, start + i * HEADS + own, share) for i in range(3)
    ]
    return (
        output, token_grad.astype(bf16), in_share, out_share, conv_weight_share,
        conv_bias_share, norm_share, gate_share, *heads,
    )


def solution(mesh):
    return jax.shard_map(
        on_device,
        mesh=mesh,
        in_specs=(
            P(("dp", "fsdp"), None),
            P(("dp", "fsdp"), None),
            P(None, ("dp", "fsdp")),
            P(None, ("dp", "fsdp")),
            P(("dp", "fsdp")),
            P(("dp", "fsdp")),
            P(("dp", "fsdp")),
            P("fsdp"),
            P("fsdp"),
            P("fsdp"),
            P(("dp", "fsdp"), None),
        ),
        out_specs=(
            P(("dp", "fsdp"), None),
            P(("dp", "fsdp"), None),
            P(("dp", "fsdp"), None),
            P(None, ("dp", "fsdp")),
            P(None, ("dp", "fsdp")),
            P(("dp", "fsdp")),
            P(("dp", "fsdp")),
            P(("dp", "fsdp")),
            P("fsdp"),
            P("fsdp"),
            P("fsdp"),
        ),
        check_vma=False,
    )
```
